32 devices in a mesh: row: 4 (over z), col: 8 (over y, x, core).
Axes of the slice: x: 2, y: 2, z: 4, core: 2. Of those that a mesh axis runs over, the one named last changes fastest.
Arguments:
- right_sides: float32 [16, 1024, 1024], P(None, 'row', 'col'), may hold values from -6 to 6
- inverse_first: float32 [1024, 1024], P(None, 'row'), may hold values from -1.4 to 1.4, as said below
- inverse_second: float32 [1024, 1024], P(None, 'row'), may hold values from -1.4 to 1.4, as said below
- column_first: float32 [15, 1024, 1024], P(None, 'row', 'col'), may hold values from -0.1875 to 0.1875
- column_second: float32 [14, 1024, 1024], P(None, 'row', 'col'), may hold values from -0.1875 to 0.1875
Outputs:
- solutions: float32 [2, 1024, 1024], P(None, None, 'col')
- updated_sides: float32 [16, 1024, 1024], P(None, 'row', 'col')
The draws below stay inside these ranges and needn't reach their ends.
Inputs may be any that keep to these rules, and one draw needn't show every extreme that they name: `inverse_first`: lower triangular; diagonal entries between 0.6 and 1.4. `inverse_second`: lower triangular; diagonal entries between 0.6 and 1.4.
All inputs are finite; a program needn't handle non-finite values.
Results may differ from the reference program's by a relative error of at most 0.000084.
Values sent between devices are 32-bit elements; how exact they have to be, the bound alone decides.
A program may use at most 128 MiB of HBM per device.

```python
import jax
import jax.numpy as jnp
from jax import lax

NB = 1024
BLOCKS = 16
R = 1024


def lower_block(key, off_values):
    key_diag = jax.random.fold_in(key, 11)
    diag_values = jax.random.uniform(key_diag, (NB,), jnp.float32, 0.6, 1.4)
    row_index = jnp.arange(NB)[:, None]
    col_index = jnp.arange(NB)[None, :]
    strict = jnp.where(row_index > col_index, off_values, 0.0)
    return strict + jnp.where(row_index == col_index, diag_values[:, None], 0.0)


def draw_inverse_first(key, part):
    key = jax.random.fold_in(key, 3)
    scale = 0.8 / NB ** 0.5
    off_values = jax.random.normal(key, (NB, NB), jnp.float32) * scale
    return lower_block(key, off_values)


def draw_inverse_second(key, part):
    key = jax.random.fold_in(key, 7)
    scale = 0.8 / NB ** 0.5
    off_values = jax.random.normal(key, (NB, NB), jnp.float32) * scale
    return lower_block(key, off_values)


def shard_levels(key, shape, pieces, low, largest):
    factor_of, own = 1.0, jax.random.fold_in(key, 6)
    for axis_at, blocks in pieces:
        steps = jnp.exp(jax.random.uniform(jax.random.fold_in(own, axis_at), (blocks,), jnp.float32, low / len(pieces), largest / len(pieces)))
        factor_of = factor_of * jnp.repeat(steps, shape[axis_at] // blocks).reshape([-1 if axis == axis_at else 1 for axis in range(len(shape))])
    return factor_of


def normal_values(key, shape, width, most, cuts=(), dtype=jnp.bfloat16):
    result = width * jax.random.normal(key, shape, jnp.float32)
    if cuts:
        result = result * shard_levels(key, shape, cuts, -0.22, 0.18)
    return jnp.clip(result, -most, most).astype(dtype)


def setup_inputs(seed: int = 0) -> dict:
    arg_keys = jax.random.split(jax.random.key(seed), 6)
    right_sides = normal_values(arg_keys[0], (BLOCKS, NB, R), 1.0, 6.0, ((1, 4), (2, 8)), jnp.float32)
    inverse_first = draw_inverse_first(jax.random.fold_in(arg_keys[5], 71), 0)
    inverse_second = draw_inverse_second(jax.random.fold_in(arg_keys[5], 71), 0)
    column_first = normal_values(arg_keys[3], (BLOCKS - 1, NB, NB), NB ** -0.5, 0.1875, ((1, 4), (2, 8)), jnp.float32)
    column_second = normal_values(arg_keys[4], (BLOCKS - 2, NB, NB), NB ** -0.5, 0.1875, ((1, 4), (2, 8)), jnp.float32)
    return {"right_sides": right_sides, "inverse_first": inverse_first, "inverse_second": inverse_second, "column_first": column_first, "column_second": column_second}


def reference(right_sides, inverse_first, inverse_second, column_first, column_second):
    highest = lax.Precision.HIGHEST
    solved_first = jnp.dot(inverse_first, right_sides[0], precision=highest, preferred_element_type=jnp.float32)
    trailing = right_sides[1:] - jnp.einsum("bij,jr->bir", column_first, solved_first, precision=highest, preferred_element_type=jnp.float32)
    after_first = jnp.concatenate([right_sides[:1], trailing], axis=0)
    solved_second = jnp.dot(inverse_second, after_first[1], precision=highest, preferred_element_type=jnp.float32)
    remainder = after_first[2:] - jnp.einsum("bij,jr->bir", column_second, solved_second, precision=highest, preferred_element_type=jnp.float32)
    updated_sides = jnp.concatenate([after_first[:2], remainder], axis=0)
    solutions = jnp.stack([solved_first, solved_second])
    return solutions, updated_sides
```

```python
import functools

import jax
import jax.numpy as jnp
from jax import lax
from jax.experimental import pallas as pl
from jax.experimental.pallas import tpu as pltpu
from jax.sharding import PartitionSpec as P

HIGHEST = lax.Precision.HIGHEST
MESH = pl.DeviceIdType.MESH
F32 = jnp.float32
BF16 = jnp.bfloat16


def split(value):
    high = value.astype(BF16)
    low = (value - high.astype(F32)).astype(BF16)
    return high, low


def product(a_high, a_low, b_high, b_low):
    dot = functools.partial(jnp.dot, preferred_element_type=F32)
    return dot(a_high, b_high) + (dot(a_high, b_low) + dot(a_low, b_high))


def kernel(
    rows, cols,
    sides, inv_one, inv_two, c_one, c_two,
    solved_out, sides_out,
    acc, inv, c1, c2, partial, partial_in, solved, other_x, other_y,
    op_high, op_low, outgoing, incoming, share_in,
    local_sem, g_send, g_recv, f_send, f_recv, o_send, o_recv,
    p_send, p_recv, b_send, b_recv, e_send, e_recv, r_send, r_recv, w_sem,
):
    nb, tile, lanes = sides.shape
    pairs = (nb - 2) // 2
    z, c = lax.axis_index("row"), lax.axis_index("col")
    core, x, y = lax.rem(c, 2), lax.rem(c // 2, 2), c // 4
    by_x, by_y, sibling = c + 2 - 4 * x, c + 4 - 8 * y, c + 1 - 2 * core
    slot_x, slot_y = 2 * x + core, 2 * y + core
    from_x, from_y = 2 * (1 - x) + core, 2 * (1 - y) + core

    def remote(src, dst, send, recv, device):
        return pltpu.make_async_remote_copy(
            src_ref=src, dst_ref=dst, send_sem=send, recv_sem=recv,
            device_id=device, device_id_type=MESH)

    load_zero = pltpu.make_async_copy(sides.at[0], acc.at[0], local_sem.at[0])
    load_inv1 = pltpu.make_async_copy(inv_one, inv.at[0], local_sem.at[1])
    load_inv2 = pltpu.make_async_copy(inv_two, inv.at[1], local_sem.at[2])
    load_rest = pltpu.make_async_copy(
        sides.at[pl.ds(1, nb - 1)], acc.at[pl.ds(1, nb - 1)], local_sem.at[3])
    runs = [
        (c_one, c1, 0, 1, slot_x),
        (c_one, c1, 1, pairs, slot_x),
        (c_two, c2, 0, pairs, slot_x),
        (c_one, c1, 1 + pairs, pairs, slot_y),
        (c_two, c2, pairs, pairs, slot_y),
    ]
    own = [
        pltpu.make_async_copy(
            src.at[pl.ds(at, n)], dst.at[pl.ds(at, n), slot], local_sem.at[4 + k])
        for k, (src, dst, at, n, slot) in enumerate(runs)]
    to_sibling = [
        remote(src.at[pl.ds(at, n)], dst.at[pl.ds(at, n), slot],
               o_send.at[k], o_recv.at[k], (z, sibling))
        for k, (src, dst, at, n, slot) in enumerate(runs)]
    load_zero.start()
    load_inv1.start()

    barrier = pltpu.get_barrier_semaphore()
    peers = [(z, by_x), (z, by_y), (z, sibling)]
    peers += [(lax.rem(z + d, rows), c) for d in range(1, rows)]
    for peer in peers:
        pl.semaphore_signal(barrier, inc=1, device_id=peer, device_id_type=MESH)
    load_rest.start()
    load_inv2.start()
    for copy in own:
        copy.start()
    pl.semaphore_wait(barrier, len(peers))

    def gather(src, dst, k, base, along_x):
        slot, device = (slot_x, by_x) if along_x else (slot_y, by_y)
        return remote(src.at[k], dst.at[k, slot],
                      g_send.at[base + k], g_recv.at[base + k], (z, device))

    def forward(dst, k, base, along_x):
        slot = from_x if along_x else from_y
        return remote(dst.at[k, slot], dst.at[k, slot],
                      f_send.at[base + k], f_recv.at[base + k], (z, sibling))

    second = nb - 1

    def of_pair(p, make):
        return [make(c_one, c1, 1 + p, 0, True), make(c_one, c1, 1 + pairs + p, 0, False),
                make(c_two, c2, p, second, True), make(c_two, c2, pairs + p, second, False)]

    def gather_pair(p):
        return of_pair(p, gather)

    def forward_pair(p):
        return of_pair(p, lambda src, dst, k, base, along: forward(dst, k, base, along))

    def start_gathers(first, last):
        @pl.loop(first, last)
        def _(p):
            for copy in gather_pair(p):
                copy.start()

    def pass_on(first, last):
        @pl.loop(first, last)
        def _(p):
            for arrived, copy in zip(gather_pair(p), forward_pair(p)):
                arrived.wait_recv()
                copy.start()

    head = gather(c_one, c1, 0, 0, True)
    head_forward = forward(c1, 0, 0, True)
    head.start()
    to_sibling[0].start()

    def partial_copy(step, d):
        k = step * (rows - 1) + d - 1
        return remote(partial.at[step, lax.rem(z + d, rows)], partial_in.at[step, d - 1],
                      p_send.at[k], p_recv.at[k], (lax.rem(z + d, rows), c))

    def block_of(step, i):
        return solved.at[step, i // 2, lax.rem(i, 2)]

    def spread_copy(step, d):
        k = step * (rows - 1) + d - 1
        return remote(block_of(step, z), block_of(step, z),
                      b_send.at[k], b_recv.at[k], (lax.rem(z + d, rows), c))

    def exchange(step):
        return [
            remote(solved.at[step, 1 - y], other_y.at[step],
                   e_send.at[2 * step], e_recv.at[2 * step], (z, by_y)),
            remote(solved.at[step, :, 1 - x], other_x.at[step],
                   e_send.at[2 * step + 1], e_recv.at[2 * step + 1], (z, by_x)),
        ]

    def multiply_out(step):
        b_high, b_low = split(acc[step])
        for d in reversed(range(rows)):
            @pl.when(z + d < rows)
            def _():
                i = z + d
                a = inv[step, pl.ds(pl.multiple_of(i * tile, tile), tile), :]
                partial[step, i] = product(*split(a), b_high, b_low)
                if d:
                    partial_copy(step, d).start()

    def collect(step):
        for d in range(1, rows):
            @pl.when(z - d >= 0)
            def _():
                partial_copy(step, d).wait_recv()
                partial[step, z] += partial_in[step, d - 1]
        solved[step, z // 2, lax.rem(z, 2)] = partial[step, z]
        for d in range(1, rows):
            spread_copy(step, d).start()

    def finish_solve(step):
        for d in range(1, rows):
            spread_copy(step, d).wait_recv()
        for copy in exchange(step):
            copy.start()
        for k in range(2):
            at = pl.ds(k * tile, tile)
            for path, mine in enumerate((solved[step, y, k], solved[step, k, x])):
                op_high[step, path, at, :lanes], op_low[step, path, at, :lanes] = split(mine)

    def finish_exchange(step):
        for path, (copy, other) in enumerate(zip(exchange(step), (other_y, other_x))):
            copy.wait_recv()
            for k in range(2):
                at = pl.ds(k * tile, tile)
                op_high[step, path, at, lanes:], op_low[step, path, at, lanes:] = split(
                    other[step, k])

    def fold(ref, k, step, path):
        a = jnp.concatenate([ref[k, s] for s in range(4)], axis=1)
        return product(*split(a), op_high[step, path], op_low[step, path])

    def share(b, along_x):
        return remote(outgoing.at[b], incoming.at[b], r_send.at[b], r_recv.at[b],
                      (z, by_y if along_x else by_x))

    def write_out(b):
        return pltpu.make_async_copy(acc.at[b], sides_out.at[b], w_sem.at[b])

    load_zero.wait()
    load_inv1.wait()
    multiply_out(0)
    start_gathers(0, STAGE[0])
    for copy in to_sibling[1:]:
        copy.start()
    write_out(0).start()
    head.wait_recv()
    head_forward.start()
    collect(0)
    start_gathers(STAGE[0], STAGE[1])
    finish_solve(0)
    pass_on(0, STAGE[2])
    load_rest.wait()
    own[0].wait()
    to_sibling[0].wait_recv()
    head_forward.wait_recv()
    finish_exchange(0)

    both = fold(c1, 0, 0, 0)
    outgoing[1] = both[:, lanes:]
    share(1, True).start()
    acc[1] -= both[:, :lanes]
    start_gathers(STAGE[1], STAGE[3])
    load_inv2.wait()
    share(1, True).wait_recv()
    acc[1] -= incoming[1]
    multiply_out(1)
    write_out(1).start()
    start_gathers(STAGE[3], pairs)
    collect(1)
    for copy in own[1:]:
        copy.wait()
    for copy in to_sibling[1:]:
        copy.wait_recv()
    finish_solve(1)
    pass_on(STAGE[2], pairs)
    finish_exchange(1)
    store_solved = pltpu.make_async_copy(solved, solved_out, share_in.at[0])
    store_solved.start()

    @pl.loop(0, pairs)
    def _(p):
        for copy in forward_pair(p):
            copy.wait_recv()
        for path in range(2):
            q = path * pairs + p
            b = 2 + q
            both = fold(c1, 1 + q, 0, path) + fold(c2, q, 1, path)
            outgoing[b] = both[:, lanes:]
            share(b, path == 0).start()
            acc[b] -= both[:, :lanes]

    @pl.loop(0, pairs)
    def _(p):
        for path in range(2):
            b = 2 + path * pairs + p
            share(b, path == 0).wait_recv()
            acc[b] -= incoming[b]
            write_out(b).start()

    head.wait_send()
    head_forward.wait_send()
    share(1, True).wait_send()
    for copy in to_sibling:
        copy.wait_send()
    for step in range(2):
        for d in range(1, rows):
            @pl.when(z + d < rows)
            def _():
                partial_copy(step, d).wait_send()
            spread_copy(step, d).wait_send()
        for copy in exchange(step):
            copy.wait_send()
    store_solved.wait()
    write_out(0).wait()
    write_out(1).wait()

    @pl.loop(0, pairs)
    def _(p):
        for copy in gather_pair(p) + forward_pair(p):
            copy.wait_send()
        for path in range(2):
            b = 2 + path * pairs + p
            share(b, path == 0).wait_send()
            write_out(b).wait()


STAGE = (2, 4, 3, 5)


def fused(rows, cols, sides, inv_one, inv_two, c_one, c_two):
    nb, tile, lanes = sides.shape
    n = inv_one.shape[0]
    chunks = c_one.shape[0] + c_two.shape[0]
    dma = pltpu.SemaphoreType.DMA
    anywhere = pl.BlockSpec(memory_space=pl.ANY)
    solved, updated = pl.pallas_call(
        functools.partial(kernel, rows, cols),
        out_shape=(
            jax.ShapeDtypeStruct((2, 2, 2, tile, lanes), F32),
            jax.ShapeDtypeStruct(sides.shape, F32),
        ),
        in_specs=[anywhere] * 5,
        out_specs=(anywhere, anywhere),
        scratch_shapes=[
            pltpu.VMEM((nb, tile, lanes), F32),
            pltpu.VMEM((2, n, tile), F32),
            pltpu.VMEM((nb - 1, 4, tile, lanes), F32),
            pltpu.VMEM((nb - 2, 4, tile, lanes), F32),
            pltpu.VMEM((2, rows, tile, lanes), F32),
            pltpu.VMEM((2, rows - 1, tile, lanes), F32),
            pltpu.VMEM((2, 2, 2, tile, lanes), F32),
            pltpu.VMEM((2, 2, tile, lanes), F32),
            pltpu.VMEM((2, 2, tile, lanes), F32),
            pltpu.VMEM((2, 2, 2 * tile, 2 * lanes), BF16),
            pltpu.VMEM((2, 2, 2 * tile, 2 * lanes), BF16),
            pltpu.VMEM((nb, tile, lanes), F32),
            pltpu.VMEM((nb, tile, lanes), F32),
            dma((1,)),
            dma((9,)),
            dma((chunks,)), dma((chunks,)),
            dma((chunks,)), dma((chunks,)),
            dma((5,)), dma((5,)),
            dma((2 * (rows - 1),)), dma((2 * (rows - 1),)),
            dma((2 * (rows - 1),)), dma((2 * (rows - 1),)),
            dma((4,)), dma((4,)),
            dma((nb,)), dma((nb,)),
            dma((nb,)),
        ],
        compiler_params=pltpu.CompilerParams(
            collective_id=0, has_side_effects=True, vmem_limit_bytes=48 * 2**20),
        cost_estimate=pl.CostEstimate(
            flops=6 * chunks * tile * n * lanes, bytes_accessed=16 * 2**20, transcendentals=0),
    )(sides, inv_one, inv_two, c_one, c_two)
    return solved.reshape(2, n, lanes), updated


def apply_inverse(inverse, rhs_block):
    local_product = jnp.dot(
        inverse, rhs_block, precision=HIGHEST, preferred_element_type=jnp.float32
    )
    return lax.psum(local_product, "row")


def fold_panel(fragment, solved):
    return jnp.einsum(
        "bij,jr->bir", fragment, solved, precision=HIGHEST, preferred_element_type=jnp.float32
    )


def update_rows(factor_panel, solved):
    return fold_panel(lax.all_gather(factor_panel, "col", axis=2, tiled=True), solved)


def on_device(right_sides, inverse_first, inverse_second, column_first, column_second):
    solved_first = apply_inverse(inverse_first, right_sides[0])
    after_first = right_sides[1:] - update_rows(column_first, solved_first)
    solved_second = apply_inverse(inverse_second, after_first[0])
    remainder = after_first[1:] - update_rows(column_second, solved_second)
    updated_sides = jnp.concatenate([right_sides[:1], after_first[:1], remainder], axis=0)
    solutions = jnp.stack([solved_first, solved_second])
    return (solutions, updated_sides)


def solution(mesh):
    placed = (
        P(None, "row", "col"),
        P(None, "row"),
        P(None, "row"),
        P(None, "row", "col"),
        P(None, "row", "col"),
    )
    rows, cols = mesh.shape["row"], mesh.shape["col"]
    local = functools.partial(fused, rows, cols) if (rows, cols) == (4, 8) else on_device
    return jax.shard_map(
        local,
        mesh=mesh,
        in_specs=placed,
        out_specs=(P(None, None, "col"), P(None, "row", "col")),
        check_vma=False,
    )
```

```python
import functools

import jax
import jax.numpy as jnp
from jax import lax
from jax.experimental import pallas as pl
from jax.experimental.pallas import tpu as pltpu
from jax.sharding import PartitionSpec as P

HIGHEST = lax.Precision.HIGHEST
MESH = pl.DeviceIdType.MESH
F32 = jnp.float32
BF16 = jnp.bfloat16


def split(value):
    high = value.astype(BF16)
    low = (value - high.astype(F32)).astype(BF16)
    return high, low


def rows_of(i, n):
    return pl.ds(pl.multiple_of(i * n, n), n)


def product(a_high, a_low, b_high, b_low):
    dot = functools.partial(jnp.dot, preferred_element_type=F32)
    return dot(a_high, b_high) + (dot(a_high, b_low) + dot(a_low, b_high))


def kernel(
    rows, cols,
    sides, inv_one, inv_two, c_one, c_two,
    solved_out, sides_out,
    acc, inv, c1, c2, partial, partial_in, solved, other_x, other_y,
    op_high, op_low, outgoing, incoming, share_in,
    local_sem, g_send, g_recv, f_send, f_recv, o_send, o_recv,
    p_send, p_recv, up_send, down_send, b_recv, e_send, e_recv, r_send, r_recv, w_sem,
):
    nb, tile, lanes = sides.shape
    pairs = (nb - 2) // 2
    z, c = lax.axis_index("row"), lax.axis_index("col")
    core, x, y = lax.rem(c, 2), lax.rem(c // 2, 2), c // 4
    by_x, by_y, sibling = c + 2 - 4 * x, c + 4 - 8 * y, c + 1 - 2 * core
    slot_x, slot_y = 2 * x + core, 2 * y + core
    from_x, from_y = 2 * (1 - x) + core, 2 * (1 - y) + core

    def remote(src, dst, send, recv, device):
        return pltpu.make_async_remote_copy(
            src_ref=src, dst_ref=dst, send_sem=send, recv_sem=recv,
            device_id=device, device_id_type=MESH)

    load_zero = pltpu.make_async_copy(sides.at[0], acc.at[0], local_sem.at[0])
    load_inv1 = pltpu.make_async_copy(inv_one, inv.at[0], local_sem.at[1])
    load_inv2 = pltpu.make_async_copy(inv_two, inv.at[1], local_sem.at[2])
    load_rest = pltpu.make_async_copy(
        sides.at[pl.ds(1, nb - 1)], acc.at[pl.ds(1, nb - 1)], local_sem.at[3])
    runs = [
        (c_one, c1, 0, 1, slot_x),
        (c_one, c1, 1, pairs, slot_x),
        (c_two, c2, 0, pairs, slot_x),
        (c_one, c1, 1 + pairs, pairs, slot_y),
        (c_two, c2, pairs, pairs, slot_y),
    ]
    own = [
        pltpu.make_async_copy(
            src.at[pl.ds(at, n)], dst.at[pl.ds(at, n), slot], local_sem.at[4 + k])
        for k, (src, dst, at, n, slot) in enumerate(runs)]
    to_sibling = [
        remote(src.at[pl.ds(at, n)], dst.at[pl.ds(at, n), slot],
               o_send.at[k], o_recv.at[k], (z, sibling))
        for k, (src, dst, at, n, slot) in enumerate(runs)]
    load_zero.start()
    load_inv1.start()

    barrier = pltpu.get_barrier_semaphore()
    peers = [(z, by_x), (z, by_y), (z, sibling)]
    peers += [(lax.rem(z + d, rows), c) for d in range(1, rows)]
    for peer in peers:
        pl.semaphore_signal(barrier, inc=1, device_id=peer, device_id_type=MESH)
    load_rest.start()
    load_inv2.start()
    for copy in own:
        copy.start()
    pl.semaphore_wait(barrier, len(peers))

    def gather(src, dst, k, base, along_x):
        slot, device = (slot_x, by_x) if along_x else (slot_y, by_y)
        return remote(src.at[k], dst.at[k, slot],
                      g_send.at[base + k], g_recv.at[base + k], (z, device))

    def forward(dst, k, base, along_x):
        slot = from_x if along_x else from_y
        return remote(dst.at[k, slot], dst.at[k, slot],
                      f_send.at[base + k], f_recv.at[base + k], (z, sibling))

    second = nb - 1

    def of_pair(p, make):
        return [make(c_one, c1, 1 + p, 0, True), make(c_one, c1, 1 + pairs + p, 0, False),
                make(c_two, c2, p, second, True), make(c_two, c2, pairs + p, second, False)]

    def gather_pair(p):
        return of_pair(p, gather)

    def forward_pair(p):
        return of_pair(p, lambda src, dst, k, base, along: forward(dst, k, base, along))

    def start_gathers(first, last):
        @pl.loop(first, last)
        def _(p):
            for copy in gather_pair(p):
                copy.start()

    def pass_on(first, last):
        @pl.loop(first, last)
        def _(p):
            for arrived, copy in zip(gather_pair(p), forward_pair(p)):
                arrived.wait_recv()
                copy.start()

    head = gather(c_one, c1, 0, 0, True)
    head_forward = forward(c1, 0, 0, True)
    head.start()
    to_sibling[0].start()

    def sum_copy(step, i):
        k = step * rows + i
        return remote(partial.at[step, i], partial_in.at[step, i],
                      p_send.at[k], p_recv.at[k], (lax.rem(z + 1, rows), c))

    def block_of(step, i):
        return solved.at[step, i // 2, lax.rem(i, 2)]

    def up_copy(step, i):
        k = step * rows + i
        return remote(block_of(step, i), block_of(step, i), up_send.at[k], b_recv.at[k],
                      (lax.rem(z + 1, rows), c))

    def down_copy(step, to):
        k = step * rows + z
        return remote(block_of(step, z), block_of(step, z), down_send.at[step * rows + to],
                      b_recv.at[k], (to, c))

    def exchange_y(step, k):
        at = 4 * step + k
        return remote(solved.at[step, 1 - y, k], other_y.at[step, k],
                      e_send.at[at], e_recv.at[at], (z, by_y))

    def exchange_x(step, k):
        at = 4 * step + 2 + k
        return remote(solved.at[step, k, 1 - x], other_x.at[step, k],
                      e_send.at[at], e_recv.at[at], (z, by_x))

    def pass_block(step, i):
        @pl.when(i // 2 == 1 - y)
        def _():
            exchange_y(step, lax.rem(i, 2)).start()

        @pl.when(lax.rem(i, 2) == 1 - x)
        def _():
            exchange_x(step, i // 2).start()

    def solve(step):
        b_high, b_low = split(acc[step])
        for i in reversed(range(rows)):
            @pl.when(z <= i)
            def _():
                a = inv[step, pl.ds(i * tile, tile), :]
                partial[step, i] = product(*split(a), b_high, b_low)

                @pl.when(z > 0)
                def _():
                    sum_copy(step, i).wait_recv()
                    partial[step, i] += partial_in[step, i]

            if i:
                @pl.when(z < i)
                def _():
                    sum_copy(step, i).start()

            @pl.when(z == i)
            def _():
                solved[step, i // 2, i % 2] = partial[step, i]
                for to in range(i):
                    down_copy(step, to).start()

            @pl.when(z > i)
            def _():
                up_copy(step, i).wait_recv()

            if i < rows - 1:
                @pl.when((z >= i) & (z < rows - 1))
                def _():
                    up_copy(step, i).start()

            @pl.when(z >= i)
            def _():
                pass_block(step, i)

    def finish_spread(step):
        for i in range(1, rows):
            @pl.when(z < i)
            def _():
                up_copy(step, i).wait_recv()
                pass_block(step, i)
        for k in range(2):
            at = pl.ds(k * tile, tile)
            for path, mine in enumerate((solved[step, y, k], solved[step, k, x])):
                op_high[step, path, at, :lanes], op_low[step, path, at, :lanes] = split(mine)

    def finish_exchange(step):
        for path, (copy, other) in enumerate(((exchange_y, other_y), (exchange_x, other_x))):
            for k in range(2):
                at = pl.ds(k * tile, tile)
                copy(step, k).wait_recv()
                op_high[step, path, at, lanes:], op_low[step, path, at, lanes:] = split(
                    other[step, k])

    def fold(ref, k, step, path):
        a = jnp.concatenate([ref[k, s] for s in range(4)], axis=1)
        return product(*split(a), op_high[step, path], op_low[step, path])

    def share(b, along_x):
        return remote(outgoing.at[b], incoming.at[b], r_send.at[b], r_recv.at[b],
                      (z, by_y if along_x else by_x))

    def write_out(b):
        return pltpu.make_async_copy(acc.at[b], sides_out.at[b], w_sem.at[b])

    load_zero.wait()
    load_inv1.wait()
    start_gathers(0, STAGE[0])
    for copy in to_sibling[1:]:
        copy.start()
    write_out(0).start()
    solve(0)
    finish_spread(0)
    start_gathers(STAGE[0], STAGE[1])
    pass_on(0, STAGE[2])
    head.wait_recv()
    head_forward.start()
    load_rest.wait()
    own[0].wait()
    to_sibling[0].wait_recv()
    head_forward.wait_recv()
    finish_exchange(0)

    both = fold(c1, 0, 0, 0)
    outgoing[1] = both[:, lanes:]
    share(1, True).start()
    acc[1] -= both[:, :lanes]
    start_gathers(STAGE[1], STAGE[3])
    load_inv2.wait()
    share(1, True).wait_recv()
    acc[1] -= incoming[1]
    start_gathers(STAGE[3], STAGE[4])
    solve(1)
    write_out(1).start()
    for copy in own[1:]:
        copy.wait()
    for copy in to_sibling[1:]:
        copy.wait_recv()
    finish_spread(1)
    start_gathers(STAGE[4], pairs)
    pass_on(STAGE[2], pairs)
    finish_exchange(1)
    store_solved = pltpu.make_async_copy(solved, solved_out, share_in.at[0])
    store_solved.start()

    @pl.loop(0, pairs)
    def _(p):
        for copy in forward_pair(p):
            copy.wait_recv()
        for path in range(2):
            q = path * pairs + p
            b = 2 + q
            both = fold(c1, 1 + q, 0, path) + fold(c2, q, 1, path)
            outgoing[b] = both[:, lanes:]
            share(b, path == 0).start()
            acc[b] -= both[:, :lanes]

    @pl.loop(0, pairs)
    def _(p):
        for path in range(2):
            b = 2 + path * pairs + p
            share(b, path == 0).wait_recv()
            acc[b] -= incoming[b]
            write_out(b).start()

    head.wait_send()
    head_forward.wait_send()
    share(1, True).wait_send()
    for copy in to_sibling:
        copy.wait_send()
    for step in range(2):
        for i in range(rows):
            @pl.when(z < i)
            def _():
                sum_copy(step, i).wait_send()

            @pl.when((z >= i) & (z < rows - 1))
            def _():
                up_copy(step, i).wait_send()

            @pl.when(z > i)
            def _():
                down_copy(step, i).wait_send()

        for k in range(2):
            exchange_y(step, k).wait_send()
            exchange_x(step, k).wait_send()
    store_solved.wait()
    write_out(0).wait()
    write_out(1).wait()

    @pl.loop(0, pairs)
    def _(p):
        for copy in gather_pair(p) + forward_pair(p):
            copy.wait_send()
        for path in range(2):
            b = 2 + path * pairs + p
            share(b, path == 0).wait_send()
            write_out(b).wait()


STAGE = (3, 4, 2, 4, 7)


def fused(rows, cols, sides, inv_one, inv_two, c_one, c_two):
    nb, tile, lanes = sides.shape
    n = inv_one.shape[0]
    chunks = c_one.shape[0] + c_two.shape[0]
    dma = pltpu.SemaphoreType.DMA
    anywhere = pl.BlockSpec(memory_space=pl.ANY)
    solved, updated = pl.pallas_call(
        functools.partial(kernel, rows, cols),
        out_shape=(
            jax.ShapeDtypeStruct((2, 2, 2, tile, lanes), F32),
            jax.ShapeDtypeStruct(sides.shape, F32),
        ),
        in_specs=[anywhere] * 5,
        out_specs=(anywhere, anywhere),
        scratch_shapes=[
            pltpu.VMEM((nb, tile, lanes), F32),
            pltpu.VMEM((2, n, tile), F32),
            pltpu.VMEM((nb - 1, 4, tile, lanes), F32),
            pltpu.VMEM((nb - 2, 4, tile, lanes), F32),
            pltpu.VMEM((2, rows, tile, lanes), F32),
            pltpu.VMEM((2, rows, tile, lanes), F32),
            pltpu.VMEM((2, 2, 2, tile, lanes), F32),
            pltpu.VMEM((2, 2, tile, lanes), F32),
            pltpu.VMEM((2, 2, tile, lanes), F32),
            pltpu.VMEM((2, 2, 2 * tile, 2 * lanes), BF16),
            pltpu.VMEM((2, 2, 2 * tile, 2 * lanes), BF16),
            pltpu.VMEM((nb, tile, lanes), F32),
            pltpu.VMEM((nb, tile, lanes), F32),
            dma((1,)),
            dma((9,)),
            dma((chunks,)), dma((chunks,)),
            dma((chunks,)), dma((chunks,)),
            dma((5,)), dma((5,)),
            dma((2 * rows,)), dma((2 * rows,)),
            dma((2 * rows,)), dma((2 * rows,)), dma((2 * rows,)),
            dma((8,)), dma((8,)),
            dma((nb,)), dma((nb,)),
            dma((nb,)),
        ],
        compiler_params=pltpu.CompilerParams(
            collective_id=0, has_side_effects=True, vmem_limit_bytes=60 * 2**20),
        cost_estimate=pl.CostEstimate(
            flops=6 * chunks * tile * n * lanes, bytes_accessed=16 * 2**20, transcendentals=0),
    )(sides, inv_one, inv_two, c_one, c_two)
    return solved.reshape(2, n, lanes), updated


def apply_inverse(inverse, rhs_block):
    local_product = jnp.dot(
        inverse, rhs_block, precision=HIGHEST, preferred_element_type=jnp.float32
    )
    return lax.psum(local_product, "row")


def fold_panel(fragment, solved):
    return jnp.einsum(
        "bij,jr->bir", fragment, solved, precision=HIGHEST, preferred_element_type=jnp.float32
    )


def update_rows(factor_panel, solved):
    return fold_panel(lax.all_gather(factor_panel, "col", axis=2, tiled=True), solved)


def on_device(right_sides, inverse_first, inverse_second, column_first, column_second):
    solved_first = apply_inverse(inverse_first, right_sides[0])
    after_first = right_sides[1:] - update_rows(column_first, solved_first)
    solved_second = apply_inverse(inverse_second, after_first[0])
    remainder = after_first[1:] - update_rows(column_second, solved_second)
    updated_sides = jnp.concatenate([right_sides[:1], after_first[:1], remainder], axis=0)
    solutions = jnp.stack([solved_first, solved_second])
    return (solutions, updated_sides)


def solution(mesh):
    placed = (
        P(None, "row", "col"),
        P(None, "row"),
        P(None, "row"),
        P(None, "row", "col"),
        P(None, "row", "col"),
    )
    rows, cols = mesh.shape["row"], mesh.shape["col"]
    local = functools.partial(fused, rows, cols) if (rows, cols) == (4, 8) else on_device
    return jax.shard_map(
        local,
        mesh=mesh,
        in_specs=placed,
        out_specs=(P(None, None, "col"), P(None, "row", "col")),
        check_vma=False,
    )
```

```python
import functools

import jax
import jax.numpy as jnp
from jax import lax
from jax.experimental import pallas as pl
from jax.experimental.pallas import tpu as pltpu
from jax.sharding import PartitionSpec as P

HIGHEST = lax.Precision.HIGHEST
MESH = pl.DeviceIdType.MESH
F32 = jnp.float32
BF16 = jnp.bfloat16


def split(value):
    high = value.astype(BF16)
    low = (value - high.astype(F32)).astype(BF16)
    return high, low


def rows_of(i, n):
    return pl.ds(pl.multiple_of(i * n, n), n)


def product(a_high, a_low, b_high, b_low):
    dot = functools.partial(jnp.dot, preferred_element_type=F32)
    return dot(a_high, b_high) + (dot(a_high, b_low) + dot(a_low, b_high))


def kernel(
    rows, cols,
    sides, inv_one, inv_two, c_one, c_two,
    solved_out, sides_out,
    acc, inv, c1, c2, partial, partial_in, solved, other_x, other_y,
    op_high, op_low, outgoing, incoming, share_in,
    local_sem, g_send, g_recv, f_send, f_recv, o_send, o_recv,
    p_send, p_recv, up_send, down_send, b_recv, e_send, e_recv, r_send, r_recv, w_sem,
):
    nb, tile, lanes = sides.shape
    pairs = (nb - 2) // 2
    z, c = lax.axis_index("row"), lax.axis_index("col")
    core, x, y = lax.rem(c, 2), lax.rem(c // 2, 2), c // 4
    by_x, by_y, sibling = c + 2 - 4 * x, c + 4 - 8 * y, c + 1 - 2 * core
    slot_x, slot_y = 2 * x + core, 2 * y + core
    from_x, from_y = 2 * (1 - x) + core, 2 * (1 - y) + core

    def remote(src, dst, send, recv, device):
        return pltpu.make_async_remote_copy(
            src_ref=src, dst_ref=dst, send_sem=send, recv_sem=recv,
            device_id=device, device_id_type=MESH)

    load_zero = pltpu.make_async_copy(sides.at[0], acc.at[0], local_sem.at[0])
    load_inv1 = pltpu.make_async_copy(inv_one, inv.at[0], local_sem.at[1])
    load_inv2 = pltpu.make_async_copy(inv_two, inv.at[1], local_sem.at[2])
    load_rest = pltpu.make_async_copy(
        sides.at[pl.ds(1, nb - 1)], acc.at[pl.ds(1, nb - 1)], local_sem.at[3])
    runs = [
        (c_one, c1, 0, 1, slot_x),
        (c_one, c1, 1, pairs, slot_x),
        (c_two, c2, 0, pairs, slot_x),
        (c_one, c1, 1 + pairs, pairs, slot_y),
        (c_two, c2, pairs, pairs, slot_y),
    ]
    own = [
        pltpu.make_async_copy(
            src.at[pl.ds(at, n)], dst.at[pl.ds(at, n), slot], local_sem.at[4 + k])
        for k, (src, dst, at, n, slot) in enumerate(runs)]
    to_sibling = [
        remote(src.at[pl.ds(at, n)], dst.at[pl.ds(at, n), slot],
               o_send.at[k], o_recv.at[k], (z, sibling))
        for k, (src, dst, at, n, slot) in enumerate(runs)]
    load_zero.start()
    load_inv1.start()

    barrier = pltpu.get_barrier_semaphore()
    peers = [(z, by_x), (z, by_y), (z, sibling)]
    peers += [(lax.rem(z + d, rows), c) for d in range(1, rows)]
    for peer in peers:
        pl.semaphore_signal(barrier, inc=1, device_id=peer, device_id_type=MESH)
    load_rest.start()
    load_inv2.start()
    for copy in own:
        copy.start()
    pl.semaphore_wait(barrier, len(peers))

    def gather(src, dst, k, base, along_x):
        slot, device = (slot_x, by_x) if along_x else (slot_y, by_y)
        return remote(src.at[k], dst.at[k, slot],
                      g_send.at[base + k], g_recv.at[base + k], (z, device))

    def forward(dst, k, base, along_x):
        slot = from_x if along_x else from_y
        return remote(dst.at[k, slot], dst.at[k, slot],
                      f_send.at[base + k], f_recv.at[base + k], (z, sibling))

    second = nb - 1

    def of_pair(p, make):
        return [make(c_one, c1, 1 + p, 0, True), make(c_one, c1, 1 + pairs + p, 0, False),
                make(c_two, c2, p, second, True), make(c_two, c2, pairs + p, second, False)]

    def gather_pair(p):
        return of_pair(p, gather)

    def forward_pair(p):
        return of_pair(p, lambda src, dst, k, base, along: forward(dst, k, base, along))

    def start_gathers(first, last):
        @pl.loop(first, last)
        def _(p):
            for copy in gather_pair(p):
                copy.start()

    def pass_on(first, last):
        @pl.loop(first, last)
        def _(p):
            for arrived, copy in zip(gather_pair(p), forward_pair(p)):
                arrived.wait_recv()
                copy.start()

    head = gather(c_one, c1, 0, 0, True)
    head_forward = forward(c1, 0, 0, True)
    head.start()
    to_sibling[0].start()

    half = tile // 2
    pieces = 2 * rows

    def sum_copy(step, j):
        k = step * pieces + j
        return remote(partial.at[step, j], partial_in.at[step, j],
                      p_send.at[k], p_recv.at[k], (lax.rem(z + 1, rows), c))

    def piece_of(step, j):
        return solved.at[step, j // 4, j // 2 % 2, j % 2]

    def up_copy(step, j):
        k = step * pieces + j
        return remote(piece_of(step, j), piece_of(step, j), up_send.at[k], b_recv.at[k],
                      (lax.rem(z + 1, rows), c))

    def down_copy(step, j, to):
        k = step * pieces + j
        return remote(piece_of(step, j), piece_of(step, j), down_send.at[k * rows + to],
                      b_recv.at[k], (to, c))

    def exchange_y(step, k, part):
        at = 8 * step + 2 * k + part
        return remote(solved.at[step, 1 - y, k, part], other_y.at[step, k, part],
                      e_send.at[at], e_recv.at[at], (z, by_y))

    def exchange_x(step, k, part):
        at = 8 * step + 4 + 2 * k + part
        return remote(solved.at[step, k, 1 - x, part], other_x.at[step, k, part],
                      e_send.at[at], e_recv.at[at], (z, by_x))

    def pass_piece(step, j):
        @pl.when(y == 1 - j // 4)
        def _():
            exchange_y(step, j // 2 % 2, j % 2).start()

        @pl.when(x == 1 - j // 2 % 2)
        def _():
            exchange_x(step, j // 4, j % 2).start()

    def solve(step):
        b_high, b_low = split(acc[step])
        for j in reversed(range(pieces)):
            holder = j // 2

            @pl.when(z <= holder)
            def _():
                a = inv[step, pl.ds(j * half, half), :]
                partial[step, j] = product(*split(a), b_high, b_low)

                @pl.when(z > 0)
                def _():
                    sum_copy(step, j).wait_recv()
                    partial[step, j] += partial_in[step, j]

            if holder:
                @pl.when(z < holder)
                def _():
                    sum_copy(step, j).start()

            @pl.when(z == holder)
            def _():
                solved[step, j // 4, j // 2 % 2, j % 2] = partial[step, j]
                for to in range(holder):
                    down_copy(step, j, to).start()

            @pl.when(z > holder)
            def _():
                up_copy(step, j).wait_recv()

            if holder < rows - 1:
                @pl.when((z >= holder) & (z < rows - 1))
                def _():
                    up_copy(step, j).start()

            @pl.when(z >= holder)
            def _():
                pass_piece(step, j)

    def finish_spread(step):
        for i in range(1, rows):
            for j in (2 * i + 1, 2 * i):
                @pl.when(z < i)
                def _():
                    up_copy(step, j).wait_recv()
                    pass_piece(step, j)
        for k in range(2):
            at = pl.ds(k * tile, tile)
            for path, mine in enumerate((solved[step, y, k], solved[step, k, x])):
                op_high[step, path, at, :lanes], op_low[step, path, at, :lanes] = split(
                    mine.reshape(tile, lanes))

    def finish_exchange(step):
        for path, (copy, other) in enumerate(((exchange_y, other_y), (exchange_x, other_x))):
            for k in range(2):
                at = pl.ds(k * tile, tile)
                copy(step, k, 1).wait_recv()
                copy(step, k, 0).wait_recv()
                op_high[step, path, at, lanes:], op_low[step, path, at, lanes:] = split(
                    other[step, k].reshape(tile, lanes))

    def fold(ref, k, step, path):
        a = jnp.concatenate([ref[k, s] for s in range(4)], axis=1)
        return product(*split(a), op_high[step, path], op_low[step, path])

    def share(b, along_x):
        return remote(outgoing.at[b], incoming.at[b], r_send.at[b], r_recv.at[b],
                      (z, by_y if along_x else by_x))

    def write_out(b):
        return pltpu.make_async_copy(acc.at[b], sides_out.at[b], w_sem.at[b])

    load_zero.wait()
    load_inv1.wait()
    start_gathers(0, STAGE[0])
    for copy in to_sibling[1:]:
        copy.start()
    write_out(0).start()
    solve(0)
    finish_spread(0)
    start_gathers(STAGE[0], STAGE[1])
    pass_on(0, STAGE[2])
    head.wait_recv()
    head_forward.start()
    load_rest.wait()
    own[0].wait()
    to_sibling[0].wait_recv()
    head_forward.wait_recv()
    finish_exchange(0)

    both = fold(c1, 0, 0, 0)
    outgoing[1] = both[:, lanes:]
    share(1, True).start()
    acc[1] -= both[:, :lanes]
    start_gathers(STAGE[1], STAGE[3])
    load_inv2.wait()
    share(1, True).wait_recv()
    acc[1] -= incoming[1]
    start_gathers(STAGE[3], STAGE[4])
    solve(1)
    write_out(1).start()
    for copy in own[1:]:
        copy.wait()
    for copy in to_sibling[1:]:
        copy.wait_recv()
    finish_spread(1)
    start_gathers(STAGE[4], pairs)
    pass_on(STAGE[2], pairs)
    finish_exchange(1)
    store_solved = pltpu.make_async_copy(solved, solved_out, share_in.at[0])
    store_solved.start()

    @pl.loop(0, pairs)
    def _(p):
        for copy in forward_pair(p):
            copy.wait_recv()
        for path in range(2):
            q = path * pairs + p
            b = 2 + q
            both = fold(c1, 1 + q, 0, path) + fold(c2, q, 1, path)
            outgoing[b] = both[:, lanes:]
            share(b, path == 0).start()
            acc[b] -= both[:, :lanes]

    @pl.loop(0, pairs)
    def _(p):
        for path in range(2):
            b = 2 + path * pairs + p
            share(b, path == 0).wait_recv()
            acc[b] -= incoming[b]
            write_out(b).start()

    head.wait_send()
    head_forward.wait_send()
    share(1, True).wait_send()
    for copy in to_sibling:
        copy.wait_send()
    for step in range(2):
        for j in range(pieces):
            holder = j // 2

            @pl.when(z < holder)
            def _():
                sum_copy(step, j).wait_send()

            @pl.when((z >= holder) & (z < rows - 1))
            def _():
                up_copy(step, j).wait_send()

            @pl.when(z == holder)
            def _():
                for to in range(holder):
                    down_copy(step, j, to).wait_send()

        for k in range(2):
            for part in range(2):
                exchange_y(step, k, part).wait_send()
                exchange_x(step, k, part).wait_send()
    store_solved.wait()
    write_out(0).wait()
    write_out(1).wait()

    @pl.loop(0, pairs)
    def _(p):
        for copy in gather_pair(p) + forward_pair(p):
            copy.wait_send()
        for path in range(2):
            b = 2 + path * pairs + p
            share(b, path == 0).wait_send()
            write_out(b).wait()


STAGE = (3, 4, 2, 4, 7)


def fused(rows, cols, sides, inv_one, inv_two, c_one, c_two):
    nb, tile, lanes = sides.shape
    n = inv_one.shape[0]
    chunks = c_one.shape[0] + c_two.shape[0]
    dma = pltpu.SemaphoreType.DMA
    anywhere = pl.BlockSpec(memory_space=pl.ANY)
    solved, updated = pl.pallas_call(
        functools.partial(kernel, rows, cols),
        out_shape=(
            jax.ShapeDtypeStruct((2, 2, 2, 2, tile // 2, lanes), F32),
            jax.ShapeDtypeStruct(sides.shape, F32),
        ),
        in_specs=[anywhere] * 5,
        out_specs=(anywhere, anywhere),
        scratch_shapes=[
            pltpu.VMEM((nb, tile, lanes), F32),
            pltpu.VMEM((2, n, tile), F32),
            pltpu.VMEM((nb - 1, 4, tile, lanes), F32),
            pltpu.VMEM((nb - 2, 4, tile, lanes), F32),
            pltpu.VMEM((2, 2 * rows, tile // 2, lanes), F32),
            pltpu.VMEM((2, 2 * rows, tile // 2, lanes), F32),
            pltpu.VMEM((2, 2, 2, 2, tile // 2, lanes), F32),
            pltpu.VMEM((2, 2, 2, tile // 2, lanes), F32),
            pltpu.VMEM((2, 2, 2, tile // 2, lanes), F32),
            pltpu.VMEM((2, 2, 2 * tile, 2 * lanes), BF16),
            pltpu.VMEM((2, 2, 2 * tile, 2 * lanes), BF16),
            pltpu.VMEM((nb, tile, lanes), F32),
            pltpu.VMEM((nb, tile, lanes), F32),
            dma((1,)),
            dma((9,)),
            dma((chunks,)), dma((chunks,)),
            dma((chunks,)), dma((chunks,)),
            dma((5,)), dma((5,)),
            dma((4 * rows,)), dma((4 * rows,)),
            dma((4 * rows,)), dma((4 * rows * rows,)), dma((4 * rows,)),
            dma((16,)), dma((16,)),
            dma((nb,)), dma((nb,)),
            dma((nb,)),
        ],
        compiler_params=pltpu.CompilerParams(
            collective_id=0, has_side_effects=True, vmem_limit_bytes=60 * 2**20),
        cost_estimate=pl.CostEstimate(
            flops=6 * chunks * tile * n * lanes, bytes_accessed=16 * 2**20, transcendentals=0),
    )(sides, inv_one, inv_two, c_one, c_two)
    return solved.reshape(2, n, lanes), updated


def apply_inverse(inverse, rhs_block):
    local_product = jnp.dot(
        inverse, rhs_block, precision=HIGHEST, preferred_element_type=jnp.float32
    )
    return lax.psum(local_product, "row")


def fold_panel(fragment, solved):
    return jnp.einsum(
        "bij,jr->bir", fragment, solved, precision=HIGHEST, preferred_element_type=jnp.float32
    )


def update_rows(factor_panel, solved):
    return fold_panel(lax.all_gather(factor_panel, "col", axis=2, tiled=True), solved)


def on_device(right_sides, inverse_first, inverse_second, column_first, column_second):
    solved_first = apply_inverse(inverse_first, right_sides[0])
    after_first = right_sides[1:] - update_rows(column_first, solved_first)
    solved_second = apply_inverse(inverse_second, after_first[0])
    remainder = after_first[1:] - update_rows(column_second, solved_second)
    updated_sides = jnp.concatenate([right_sides[:1], after_first[:1], remainder], axis=0)
    solutions = jnp.stack([solved_first, solved_second])
    return (solutions, updated_sides)


def solution(mesh):
    placed = (
        P(None, "row", "col"),
        P(None, "row"),
        P(None, "row"),
        P(None, "row", "col"),
        P(None, "row", "col"),
    )
    rows, cols = mesh.shape["row"], mesh.shape["col"]
    local = functools.partial(fused, rows, cols) if (rows, cols) == (4, 8) else on_device
    return jax.shard_map(
        local,
        mesh=mesh,
        in_specs=placed,
        out_specs=(P(None, None, "col"), P(None, "row", "col")),
        check_vma=False,
    )
```
